32 devices in a mesh: wave: 8 (over z, x), dof: 4 (over y, core).
Axes of the slice: x: 2, y: 2, z: 4, core: 2. Of those that a mesh axis runs over, the one named last changes fastest.
Arguments:
- green: bfloat16 [2, 2048, 512, 512], P(None, 'wave', None, 'dof'), may hold values from -0.25 to 0.25
- rough: float32 [2, 2048, 512], P(None, 'wave'), may hold values from -6 to 6
- axle_pos: int32 [128, 32], replicated, may hold values from 0 to 2047
- axle_load: float32 [128, 32], replicated, may hold values from 0.5 to 1.5
- rows: int32 [1024, 16], replicated, may hold values from 0 to 2047
- counts: int32 [1024], replicated, may hold values from 1 to 16, as said below
- coupling: bfloat16 [1024, 512], P(None, 'dof'), may hold values from -0.25 to 0.25
Outputs:
- response: float32 [1024, 128], P('dof', 'wave')
The draws below stay inside these ranges and needn't reach their ends.
Inputs may be any that keep to these rules, and one draw needn't show every extreme that they name: Building b uses its first counts[b] stations; some building uses all 16.
All inputs are finite; a program needn't handle non-finite values.
Results may differ from the reference program's by a relative error of at most 0.005.
Values may be sent and summed in bfloat16 or wider, within the bound.
No kernel may reach another device: no remote copies, remote signals or barrier semaphores. Data moves between devices by JAX's collectives and lax.ppermute only.
A program may use at most 320 MiB of HBM per device.

```python
import math
import jax
import jax.numpy as jnp
from jax import lax

K = 2048
NDOF = 512
NC = 128
AXLES = 32
NB = 1024
RMAX = 16


def draw_counts(key, part):
    first_key, second_key = jax.random.split(jax.random.fold_in(key, 17))
    values = jax.random.randint(first_key, (NB,), 1, RMAX + 1)
    chosen = jax.random.randint(second_key, (), 0, NB)
    return values.at[chosen].set(RMAX).astype(jnp.int32)


def plant(values, key, low, high):
    dims = values.shape
    place = [jax.random.randint(jax.random.fold_in(key, axis), (), 0, dims[axis]) for axis in range(len(dims))]
    values = values.at[tuple(place)].set(low)
    longest = dims.index(max(dims))
    place[longest] = (place[longest] + 1) % dims[longest]
    return values.at[tuple(place)].set(high)


def steps_of(key, shape, pieces, smallest, top_value):
    def one(dim, shards_of):
        draws = jax.random.uniform(jax.random.fold_in(jax.random.fold_in(key, 6), dim), (shards_of,), jnp.float32, smallest / len(pieces), top_value / len(pieces))
        return jnp.repeat(jnp.exp(draws), shape[dim] // shards_of).reshape((-1,) + (1,) * (len(shape) - dim - 1))

    loudness = one(*pieces[0])
    for cut in pieces[1:]:
        loudness = loudness * one(*cut)
    return loudness


def noise(own_key, shape, width, reach, pieces=(), held_as=jnp.bfloat16):
    level = steps_of(own_key, shape, pieces, -0.22, 0.18) if pieces else 1.0
    array = jax.random.normal(own_key, shape, jnp.float32) * width * level
    return jnp.minimum(jnp.maximum(array, -reach), reach).astype(held_as)


def setup_inputs(seed: int = 0) -> dict:
    seeds = jax.random.split(jax.random.key(seed), 8)
    return {
        "green": noise(seeds[0], (2, K, NDOF, NDOF), NDOF ** -0.5, 0.25, ((1, 8), (3, 4))),
        "rough": noise(seeds[1], (2, K, NDOF), 1.0, 6.0, ((1, 8),), jnp.float32),
        "axle_pos": plant(jax.random.randint(seeds[2], (NC, AXLES), 0, K), jax.random.fold_in(seeds[2], 1), 0, K - 1).astype(jnp.int32),
        "axle_load": jnp.clip(jax.random.uniform(seeds[3], (NC, AXLES), jnp.float32, 0.5, 1.5), 0.5, 1.5),
        "rows": plant(jax.random.randint(seeds[4], (NB, RMAX), 0, K), jax.random.fold_in(seeds[4], 1), 0, K - 1).astype(jnp.int32),
        "counts": draw_counts(jax.random.fold_in(seeds[7], 71), 0),
        "coupling": noise(seeds[6], (NB, NDOF), NDOF ** -0.5, 0.25, ((1, 4),)),
    }


def make_table():
    stations = jnp.arange(K, dtype=jnp.int32)
    product = stations[:, None] * stations[None, :] % K
    angle = product.astype(jnp.float32) * (2.0 * math.pi / K)
    scale = 1.0 / math.sqrt(K)
    table = jnp.stack([jnp.cos(angle) * scale, -jnp.sin(angle) * scale], axis=2)
    return table.reshape(K, 2 * K).astype(jnp.bfloat16)

def reference(green, rough, axle_pos, axle_load, rows, counts, coupling):
    waves = jnp.arange(K, dtype=jnp.int32)
    product = waves[:, None, None] * axle_pos[None, :, :] % K
    angle = product.astype(jnp.float32) * (2.0 * math.pi / K)
    norm_axle = 1.0 / math.sqrt(AXLES)
    phase_re = lax.optimization_barrier(jnp.sum(axle_load[None] * jnp.cos(angle), axis=2)) * norm_axle
    phase_im = -lax.optimization_barrier(jnp.sum(axle_load[None] * jnp.sin(angle), axis=2)) * norm_axle
    force_re = rough[0][:, :, None] * phase_re[:, None, :] - rough[1][:, :, None] * phase_im[:, None, :]
    force_im = rough[0][:, :, None] * phase_im[:, None, :] + rough[1][:, :, None] * phase_re[:, None, :]
    force = jnp.concatenate([force_re, force_im], axis=2).astype(jnp.bfloat16)
    case_count = axle_pos.shape[0]

    def one_wave(operands):
        green_one, force_one = operands
        prod_real = jnp.dot(green_one[0].T, force_one, preferred_element_type=jnp.float32)
        prod_imag = jnp.dot(green_one[1].T, force_one, preferred_element_type=jnp.float32)
        spec_re = prod_real[:, :case_count] - prod_imag[:, case_count:]
        spec_im = prod_real[:, case_count:] + prod_imag[:, :case_count]
        return jnp.stack([spec_re, spec_im], axis=0).astype(jnp.bfloat16)
    spectra = lax.map(one_wave, (jnp.transpose(green, (1, 0, 2, 3)), force))
    table = make_table()
    flat = spectra.reshape(K * 2, NDOF * case_count)
    field = jnp.dot(table, flat, preferred_element_type=jnp.float32)
    slots = (jnp.arange(RMAX, dtype=jnp.int32)[None, :] < counts[:, None]).astype(jnp.float32)
    building_ids = jnp.broadcast_to(jnp.arange(NB, dtype=jnp.int32)[:, None], (NB, RMAX))
    occupancy = jnp.zeros((NB, K), jnp.float32).at[building_ids, rows].add(slots).astype(jnp.bfloat16)
    gathered = jnp.dot(occupancy.astype(jnp.float32), field, precision=lax.Precision.HIGHEST, preferred_element_type=jnp.float32).reshape(NB, NDOF, case_count)
    summed = jnp.einsum('bi,bic->bc', coupling.astype(jnp.float32), gathered, precision=lax.Precision.HIGHEST)
    return summed / counts.astype(jnp.float32)[:, None]
```

```python
import functools
import math

import jax
import jax.numpy as jnp
import numpy as np
from jax import lax
from jax.experimental import pallas as pl
from jax.experimental.pallas import tpu as pltpu
from jax.sharding import PartitionSpec as P

K = 2048
LOW = 128
HIGH = K // LOW
GROUP = 256
STEP = 8
SLOTS = 16

F32 = jnp.float32
BF16 = jnp.bfloat16


def dot_nn(a, b):
    return lax.dot_general(a, b, (((1,), (0,)), ((), ())), preferred_element_type=F32)


def dot_nt(a, b):
    return lax.dot_general(a, b, (((1,), (1,)), ((), ())), preferred_element_type=F32)


def split(x):
    hi = x.astype(BF16)
    return hi, (x - hi.astype(F32)).astype(BF16)


def iota(shape, axis):
    return lax.broadcasted_iota(jnp.int32, shape, axis)


def wave_block(wave_count):
    return min(128, wave_count)


def factor_tables(wave_size, wave_count):
    block = wave_block(wave_count)

    def one(stations, scale):
        waves = np.arange(wave_size * wave_count).reshape(wave_size, 1, wave_count // block, block)
        angle = (waves * stations[None, :, None, None] % K) * (2.0 * np.pi / K)
        both = np.stack([np.cos(angle), -np.sin(angle)], axis=3) * scale
        return both.reshape(wave_size, len(stations), 2 * wave_count).astype(np.float32)

    return one(np.arange(LOW), 1.0 / math.sqrt(K)), one(np.arange(HIGH) * LOW, 1.0)[:, :, None]


def one_hot_rows(key, weights):
    parts = [jnp.where(key == float(h), w, 0.0) for w in weights for h in range(HIGH)]
    return jnp.concatenate(parts, axis=0).astype(BF16)


def spread(values, per_item):
    items = GROUP // per_item
    shape = (values.shape[0], GROUP)
    own = iota(shape, 1) // per_item == iota(shape, 0) % items
    copies = jnp.where(
        iota((per_item, GROUP), 1) % per_item == iota((per_item, GROUP), 0), 1.0, 0.0
    ).astype(BF16)
    return dot_nn(values.astype(BF16), copies), own


def kernel(
    sizes,
    green,
    rough,
    axle_pos,
    axle_load,
    rows,
    counts,
    coupling,
    low_table,
    high_table,
    out,
    ring,
    rough_v,
    pos_v,
    load_v,
    rows_v,
    counts_v,
    coupling_v,
    low_v,
    high_v,
    table_hi,
    table_lo,
    key_v,
    low_key_v,
    occupancy,
    weights_v,
    loads,
    phase_v,
    g_v,
    total,
    small_sem,
    ring_sem,
):
    wave_size, dof_size = sizes
    wave_count, _, resp = green.shape[1:]
    slot_count, building_count = rows.shape
    axle_count, case_count = axle_pos.shape
    block = wave_block(wave_count)
    blocks = wave_count // block
    steps = wave_count // STEP
    wave = lax.axis_index("wave")

    small = [
        pltpu.make_async_copy(src, dst, small_sem.at[i])
        for i, (src, dst) in enumerate(
            [
                (low_table.at[wave], low_v),
                (high_table.at[wave], high_v),
                (rows, rows_v),
                (counts, counts_v),
                (axle_pos, pos_v),
                (axle_load, load_v),
                (coupling, coupling_v),
                (rough, rough_v),
            ]
        )
    ]
    for copy in small:
        copy.start()

    def green_copy(step, slot):
        return pltpu.make_async_copy(
            green.at[:, pl.ds(step * STEP, STEP)], ring.at[slot], ring_sem.at[slot]
        )

    held = min(SLOTS, steps)
    for step in range(held):
        green_copy(step, step).start()
    for copy in small:
        copy.wait()

    @pl.loop(0, HIGH)
    def _(h):
        at = pl.ds(pl.multiple_of(h * LOW, LOW), LOW)
        for q in range(blocks):
            re = slice(2 * q * block, (2 * q + 1) * block)
            im = slice((2 * q + 1) * block, (2 * q + 2) * block)
            low_re, low_im = low_v[:, re], low_v[:, im]
            high_re, high_im = high_v[h, :, re], high_v[h, :, im]
            table_hi[at, re], table_lo[at, re] = split(low_re * high_re - low_im * high_im)
            table_hi[at, im], table_lo[at, im] = split(low_re * high_im + low_im * high_re)

    for k in range(building_count // 128):
        at = slice(128 * k, 128 * (k + 1))
        x = rows_v[:, at]
        valid = iota((slot_count, 128), 0) < counts_v[k : k + 1, :]
        high, own = spread(jnp.where(valid, x // LOW, -1).astype(F32).T, slot_count)
        low, _ = spread((x % LOW).astype(F32).T, slot_count)
        key_v[at, :] = jnp.where(own, high, -1.0)
        low_key_v[at, :] = jnp.where(own, low, 0.0)

    def low_rows(low):
        row = jnp.sum(low, axis=0, keepdims=True)
        return jnp.where(row == iota((LOW, GROUP), 0).astype(F32), 1.0, 0.0).astype(BF16)

    items = GROUP // slot_count

    @pl.loop(0, building_count // items, unroll=4)
    def _(g):
        at = pl.ds(pl.multiple_of(g * items, items), items)
        found = dot_nt(one_hot_rows(key_v[at, :], [1.0]), low_rows(low_key_v[at, :]))
        for h in range(HIGH):
            occupancy[at, h * LOW : (h + 1) * LOW] = found[h * items : (h + 1) * items].astype(BF16)

    @pl.loop(0, building_count // 256)
    def _(r):
        at = pl.ds(pl.multiple_of(r * 256, 256), 256)
        weights_v[at, :] = dot_nn(occupancy[at, :], table_hi[...])

    x = pos_v[...]
    high, own = spread((x // LOW).astype(F32).T, axle_count)
    low, _ = spread((x % LOW).astype(F32).T, axle_count)
    high, low = jnp.where(own, high, -1.0), jnp.where(own, low, 0.0)
    load_parts = [spread(part.astype(F32), axle_count)[0] for part in split(load_v[...].T)]
    items_c = GROUP // axle_count
    for g in range(case_count // items_c):
        at = slice(g * items_c, (g + 1) * items_c)
        found = dot_nt(
            one_hot_rows(high[at], [part[at] for part in load_parts]), low_rows(low[at])
        )
        found = found[: HIGH * items_c] + found[HIGH * items_c :]
        for h in range(HIGH):
            loads[at, h * LOW : (h + 1) * LOW] = found[h * items_c : (h + 1) * items_c]
    load_hi, load_lo = split(loads[...])
    phase = (
        dot_nn(load_hi, table_hi[...]) + dot_nn(load_lo, table_hi[...]) + dot_nn(load_hi, table_lo[...])
    ) * math.sqrt(K / axle_count)
    phase_hi, phase_lo = split(phase)
    phase_v[:case_count, :] = phase_hi
    phase_v[case_count:, :] = phase_lo

    def one_step(step, block_start):
        slot = lax.rem(step, held)
        green_copy(step, slot).wait()
        at = pl.ds(pl.multiple_of(step * STEP, STEP), STEP)
        re_hi, re_lo = split(rough_v[0, at, :])
        im_hi, im_lo = split(rough_v[1, at, :])
        left = jnp.concatenate(
            [
                jnp.concatenate([a.astype(F32), b.astype(F32)], axis=1)
                for a, b in ((re_hi, -im_hi), (im_hi, re_hi), (re_lo, -im_lo), (im_lo, re_lo))
            ],
            axis=0,
        ).astype(BF16)
        rank = iota((STEP, resp), 0)
        g_re = jnp.zeros((STEP, resp), F32)
        g_im = jnp.zeros((STEP, resp), F32)
        for k in range(STEP):
            right = jnp.concatenate([ring[slot, 0, k], ring[slot, 1, k]], axis=0)
            prod = dot_nn(left, right)
            g_re = jnp.where(rank == k, prod[:STEP] + prod[2 * STEP : 3 * STEP], g_re)
            g_im = jnp.where(rank == k, prod[STEP : 2 * STEP] + prod[3 * STEP :], g_im)
        row = step * STEP - block_start
        g_v[pl.ds(pl.multiple_of(row, STEP), STEP), :] = g_re
        g_v[pl.ds(pl.multiple_of(block + row, STEP), STEP), :] = g_im

        @pl.when(step + held < steps)
        def _():
            green_copy(step + held, slot).start()

    owned_cases = case_count // wave_size
    owned_buildings = building_count // dof_size
    per_tile = owned_buildings // 128
    for q in range(blocks):

        @pl.loop(q * block // STEP, (q + 1) * block // STEP)
        def _(step):
            one_step(step, q * block)

        g_both = jnp.concatenate(split(g_v[...]), axis=1)
        re = slice(2 * q * block, (2 * q + 1) * block)
        im = slice((2 * q + 1) * block, (2 * q + 2) * block)
        phase_q = phase_v[:, 2 * q * block : (2 * q + 2) * block]
        for d in range(dof_size):
            at = slice(d * owned_buildings, (d + 1) * owned_buildings)
            coupling_d = coupling_v[at, :]
            h = dot_nt(jnp.concatenate([coupling_d, coupling_d], axis=1), g_both)
            h_re, h_im = h[:, :block], h[:, block:]
            w_re, w_im = weights_v[at, re], weights_v[at, im]
            both = jnp.concatenate([w_re * h_re + w_im * h_im, w_im * h_re - w_re * h_im], axis=1)
            both_hi, both_lo = split(both)
            prod = dot_nt(phase_q, both_hi)
            part = prod[:case_count] + prod[case_count:] + dot_nt(phase_q[:case_count], both_lo)
            if q:
                part = part + total[:, at]
            if q < blocks - 1:
                total[:, at] = part
                continue
            count = jnp.concatenate(
                [counts_v[d * per_tile + t : d * per_tile + t + 1, :] for t in range(per_tile)], axis=1
            )
            part = part / count.astype(F32)
            for w in range(wave_size):
                out[w * dof_size + d] = part[w * owned_cases : (w + 1) * owned_cases].astype(BF16)


def body(green, rough, axle_pos, axle_load, rows, counts, coupling):
    wave_size = lax.axis_size("wave")
    dof_size = lax.axis_size("dof")
    wave_count, force_count, resp = green.shape[1:]
    building_count, slot_count = rows.shape
    case_count, axle_count = axle_pos.shape
    low_table, high_table = factor_tables(wave_size, wave_count)
    held = min(SLOTS, wave_count // STEP)
    owned = (case_count // wave_size, building_count // dof_size)
    any_spec = pl.BlockSpec(memory_space=pl.ANY)
    partial_sum = pl.pallas_call(
        functools.partial(kernel, (wave_size, dof_size)),
        out_shape=jax.ShapeDtypeStruct((wave_size * dof_size, *owned), BF16),
        in_specs=[any_spec] * 9,
        out_specs=pl.BlockSpec(memory_space=pltpu.VMEM),
        scratch_shapes=[
            pltpu.VMEM((held, 2, STEP, force_count, resp), BF16),
            pltpu.VMEM(rough.shape, F32),
            pltpu.VMEM((axle_count, case_count), jnp.int32),
            pltpu.VMEM((axle_count, case_count), F32),
            pltpu.VMEM((slot_count, building_count), jnp.int32),
            pltpu.VMEM((building_count // 128, 128), jnp.int32),
            pltpu.VMEM(coupling.shape, BF16),
            pltpu.VMEM(low_table.shape[1:], F32),
            pltpu.VMEM(high_table.shape[1:], F32),
            pltpu.VMEM((K, 2 * wave_count), BF16),
            pltpu.VMEM((K, 2 * wave_count), BF16),
            pltpu.VMEM((building_count, GROUP), F32),
            pltpu.VMEM((building_count, GROUP), F32),
            pltpu.VMEM((building_count, K), BF16),
            pltpu.VMEM((building_count, 2 * wave_count), F32),
            pltpu.VMEM((case_count, K), F32),
            pltpu.VMEM((2 * case_count, 2 * wave_count), BF16),
            pltpu.VMEM((2 * wave_block(wave_count), resp), F32),
            pltpu.VMEM((case_count, building_count), F32),
            pltpu.SemaphoreType.DMA((8,)),
            pltpu.SemaphoreType.DMA((held,)),
        ],
        compiler_params=pltpu.CompilerParams(vmem_limit_bytes=60 * 1024 * 1024),
    )(
        green,
        rough,
        axle_pos.T,
        axle_load.T,
        rows.T,
        counts.reshape(building_count // 128, 128),
        coupling,
        jnp.asarray(low_table),
        jnp.asarray(high_table),
    )
    arrived = lax.all_to_all(partial_sum, ("wave", "dof"), 0, 0)
    return jnp.sum(arrived.astype(F32), axis=0).T


def solution(mesh):
    in_specs = (
        P(None, "wave", None, "dof"),
        P(None, "wave", None),
        P(),
        P(),
        P(),
        P(),
        P(None, "dof"),
    )
    out_specs = P("dof", "wave")
    return jax.shard_map(body, mesh=mesh, in_specs=in_specs, out_specs=out_specs, check_vma=False)
```

```python
import functools
import math

import jax
import jax.numpy as jnp
import numpy as np
from jax import lax
from jax.experimental import pallas as pl
from jax.experimental.pallas import tpu as pltpu
from jax.sharding import PartitionSpec as P

K = 2048
HALF = K // 2
LOW = 128
HIGH = HALF // LOW
GROUP = 256
STEP = 8
AHEAD = 4

F32 = jnp.float32
BF16 = jnp.bfloat16


def dot_nn(a, b):
    return lax.dot_general(a, b, (((1,), (0,)), ((), ())), preferred_element_type=F32)


def dot_nt(a, b):
    return lax.dot_general(a, b, (((1,), (1,)), ((), ())), preferred_element_type=F32)


def split(x):
    hi = x.astype(BF16)
    return hi, (x - hi.astype(F32)).astype(BF16)


def iota(shape, axis):
    return lax.broadcasted_iota(jnp.int32, shape, axis)


def factor_tables(wave_size, wave_count):
    block = wave_count // 2

    def one(stations, scale):
        waves = np.arange(wave_size * wave_count).reshape(wave_size, 1, block, 2)
        waves = np.moveaxis(waves, 3, 2)
        angle = (waves * stations[None, :, None, None] % K) * (2.0 * np.pi / K)
        both = np.stack([np.cos(angle), -np.sin(angle)], axis=3) * scale
        return both.reshape(wave_size, len(stations), 2 * wave_count).astype(np.float32)

    return one(np.arange(LOW), 1.0 / math.sqrt(K)), one(np.arange(HIGH) * LOW, 1.0)


def one_hot_rows(key, weights, dtype):
    zero = jnp.zeros(key.shape, dtype)
    parts = [
        jnp.where(key == jnp.full(key.shape, h, dtype), w, zero) for w in weights for h in range(HIGH)
    ]
    return jnp.concatenate(parts, axis=0)


def low_rows(row, dtype):
    shape = (LOW, GROUP)
    hit = iota(shape, 0).astype(F32).astype(dtype) == jnp.broadcast_to(row, shape)
    return jnp.where(hit, jnp.ones(shape, dtype), jnp.zeros(shape, dtype))


def spread(values, per_item):
    copies = jnp.where(
        iota((per_item, GROUP), 1) % per_item == iota((per_item, GROUP), 0), 1.0, 0.0
    ).astype(BF16)
    shape = (values.shape[0], GROUP)
    own = iota(shape, 1) // per_item == iota(shape, 0) % (GROUP // per_item)
    return jnp.where(own, dot_nn(values.astype(BF16), copies), 0.0)


def station_parts(x):
    top = x >= HALF
    sign = jnp.where(top, -1.0, 1.0)
    high = lax.shift_right_logical(x, LOW.bit_length() - 1) & (HIGH - 1)
    return sign, (high + 1).astype(F32), (x & (LOW - 1)).astype(F32)


def kernel(
    sizes,
    green,
    rough,
    axle_pos,
    axle_load,
    rows,
    counts,
    coupling,
    low_table,
    high_table,
    out,
    ring,
    rough_v,
    pos_v,
    load_v,
    rows_v,
    counts_v,
    coupling_v,
    low_v,
    high_v,
    table_hi,
    table_lo,
    key_v,
    sign_v,
    low_key_v,
    occupancy,
    weights_v,
    loads,
    phase_v,
    g_v,
    total,
    small_sem,
    ring_sem,
):
    wave_size, dof_size = sizes
    block, _, _, resp = green.shape[1:]
    slot_count, building_count = rows.shape
    axle_count, case_count = axle_pos.shape
    steps = 2 * block // STEP
    held = steps // 2
    slots = ring.shape[0]
    wave = lax.axis_index("wave")

    small = [
        pltpu.make_async_copy(src, dst, small_sem.at[i])
        for i, (src, dst) in enumerate(
            [
                (rows, rows_v),
                (counts, counts_v),
                (low_table.at[wave], low_v),
                (high_table.at[wave], high_v),
                (axle_pos, pos_v),
                (axle_load, load_v),
                (coupling, coupling_v),
            ]
            + [
                (rough.at[:, :, t * 128 : (t + 1) * 128], rough_v.at[t])
                for t in range(rough_v.shape[0])
            ]
        )
    ]
    for copy in small:
        copy.start()

    def green_copy(step):
        slot = lax.rem(step, slots)
        per_block = steps // 2
        at = pl.ds(lax.rem(step, per_block) * STEP, STEP)
        return pltpu.make_async_copy(
            green.at[:, at, step // per_block], ring.at[slot], ring_sem.at[slot]
        )

    for step in range(held):
        green_copy(jnp.int32(step)).start()
    for copy in small[:2]:
        copy.wait()

    items = GROUP // slot_count
    for k in range(building_count // 128):
        at = slice(128 * k, 128 * (k + 1))
        sign, high, low = station_parts(rows_v[:, at])
        used = iota((slot_count, 128), 0) < counts_v[k : k + 1, :]
        key_v[at, :] = spread(jnp.where(used, high, 0.0).T, slot_count).astype(BF16)
        sign_v[at, :] = spread(sign.T, slot_count).astype(BF16)
        groups = 128 // items
        member = jnp.where(iota((groups, 128), 1) // items == iota((groups, 128), 0), 1.0, 0.0)
        low_key_v[groups * k : groups * (k + 1), :] = dot_nn(
            member.astype(BF16), spread(low.T, slot_count).astype(BF16)
        )

    @pl.loop(0, building_count // (8 * items))
    def _(r):
        low_eight = low_key_v[pl.ds(pl.multiple_of(r * 8, 8), 8), :]
        for k in range(8):
            at = pl.ds(pl.multiple_of((r * 8 + k) * items, items), items)
            key = key_v[at, :] - jnp.ones((items, GROUP), BF16)
            hot = one_hot_rows(key, [jnp.ones((items, GROUP), BF16), sign_v[at, :]], BF16)
            low = low_eight[k : k + 1, :].astype(BF16)
            found = dot_nt(hot, low_rows(low, BF16)).astype(BF16)
            for h in range(HIGH):
                for top in range(2):
                    row = (top * HIGH + h) * items
                    occupancy[top, at, h * LOW : (h + 1) * LOW] = found[row : row + items]

    for copy in small[2:6]:
        copy.wait()

    for h in range(HIGH):
        at = slice(h * LOW, (h + 1) * LOW)
        for q in range(2):
            re = slice(2 * q * block, (2 * q + 1) * block)
            im = slice((2 * q + 1) * block, (2 * q + 2) * block)
            low_re, low_im = low_v[:, re], low_v[:, im]
            high_re, high_im = high_v[h : h + 1, re], high_v[h : h + 1, im]
            table_hi[at, re], table_lo[at, re] = split(low_re * high_re - low_im * high_im)
            table_hi[at, im], table_lo[at, im] = split(low_re * high_im + low_im * high_re)

    for step in range(held, held + AHEAD):
        green_copy(jnp.int32(step)).start()

    @pl.loop(0, building_count // 256)
    def _(r):
        at = pl.ds(pl.multiple_of(r * 256, 256), 256)
        for q in range(2):
            cols = slice(2 * q * block, (2 * q + 2) * block)
            weights_v[at, cols] = dot_nn(occupancy[q, at, :], table_hi[:, cols])

    sign, high, low = station_parts(pos_v[...])
    high = spread(high.T, axle_count) - 1.0
    low = spread(low.T, axle_count)
    load_parts = []
    for part in split(load_v[...]):
        load_parts += [part.astype(F32), sign * part.astype(F32)]
    load_parts = [spread(part.T, axle_count) for part in load_parts]
    items_c = GROUP // axle_count
    for g in range(case_count // items_c):
        at = slice(g * items_c, (g + 1) * items_c)
        hot = one_hot_rows(high[at], [part[at] for part in load_parts], F32)
        row = jnp.sum(low[at], axis=0, keepdims=True)
        found = dot_nt(hot.astype(BF16), low_rows(row, F32).astype(BF16))
        found = found[: 2 * HIGH * items_c] + found[2 * HIGH * items_c :]
        for top in range(2):
            for h in range(HIGH):
                row = (top * HIGH + h) * items_c
                loads[top, at, h * LOW : (h + 1) * LOW] = found[row : row + items_c]
    for q in range(2):
        cols = slice(2 * q * block, (2 * q + 2) * block)
        load_hi, load_lo = split(loads[q])
        phase = (
            dot_nn(load_hi, table_hi[:, cols])
            + dot_nn(load_lo, table_hi[:, cols])
            + dot_nn(load_hi, table_lo[:, cols])
        ) * math.sqrt(K / axle_count)
        phase_v[:case_count, cols], phase_v[case_count:, cols] = split(phase)

    for copy in small[6:]:
        copy.wait()

    def pump(step):
        green_copy(step).wait()

        @pl.when(step + AHEAD < steps)
        def _():
            green_copy(step + AHEAD).start()

    def one_step(step, q):
        slot = lax.rem(step, slots)
        row = pl.multiple_of((step - q * (steps // 2)) * STEP, STEP)
        at = pl.ds(2 * row + q, STEP, stride=2)
        rough_re, rough_im = (
            jnp.concatenate([rough_v[t, part, at, :] for t in range(rough_v.shape[0])], axis=1)
            for part in range(2)
        )
        re_hi, re_lo = split(rough_re)
        im_hi, im_lo = split(rough_im)
        left = jnp.concatenate(
            [
                jnp.concatenate([a.astype(F32), b.astype(F32)], axis=1)
                for a, b in ((re_hi, -im_hi), (im_hi, re_hi), (re_lo, -im_lo), (im_lo, re_lo))
            ],
            axis=0,
        ).astype(BF16)
        rank = iota((STEP, resp), 0)
        g_re = jnp.zeros((STEP, resp), F32)
        g_im = jnp.zeros((STEP, resp), F32)
        for k in range(STEP):
            right = jnp.concatenate([ring[slot, 0, k], ring[slot, 1, k]], axis=0)
            prod = dot_nn(left, right)
            g_re = jnp.where(rank == k, prod[:STEP] + prod[2 * STEP : 3 * STEP], g_re)
            g_im = jnp.where(rank == k, prod[STEP : 2 * STEP] + prod[3 * STEP :], g_im)
        g_v[pl.ds(row, STEP), :] = g_re
        g_v[pl.ds(block + row, STEP), :] = g_im

    for step in range(held):
        green_copy(jnp.int32(step)).wait()

    owned_cases = case_count // wave_size
    owned_buildings = building_count // dof_size
    per_tile = owned_buildings // 128
    for q in range(2):

        @pl.loop(q * steps // 8, (q + 1) * steps // 8)
        def _(r):
            for k in range(4):
                if k % 2:
                    pump(held + 2 * r + k // 2)
                one_step(4 * r + k, q)

        g_both = jnp.concatenate(split(g_v[...]), axis=1)
        re = slice(2 * q * block, (2 * q + 1) * block)
        im = slice((2 * q + 1) * block, (2 * q + 2) * block)
        phase_q = phase_v[:, 2 * q * block : (2 * q + 2) * block]
        for d in range(dof_size):
            at = slice(d * owned_buildings, (d + 1) * owned_buildings)
            coupling_d = coupling_v[at, :]
            h = dot_nt(jnp.concatenate([coupling_d, coupling_d], axis=1), g_both)
            h_re, h_im = h[:, :block], h[:, block:]
            w_re, w_im = weights_v[at, re], weights_v[at, im]
            both = jnp.concatenate([w_re * h_re + w_im * h_im, w_im * h_re - w_re * h_im], axis=1)
            both_hi, both_lo = split(both)
            prod = dot_nt(phase_q, both_hi)
            part = prod[:case_count] + prod[case_count:] + dot_nt(phase_q[:case_count], both_lo)
            if q == 0:
                total[:, at] = part
                continue
            count = jnp.concatenate(
                [counts_v[d * per_tile + t : d * per_tile + t + 1, :] for t in range(per_tile)], axis=1
            )
            part = (total[:, at] + part) * (1.0 / count.astype(F32))
            for w in range(wave_size):
                out[w * dof_size + d] = part[w * owned_cases : (w + 1) * owned_cases].astype(BF16)


def body(green, rough, axle_pos, axle_load, rows, counts, coupling):
    wave_size = lax.axis_size("wave")
    dof_size = lax.axis_size("dof")
    _, wave_count, force_count, resp = green.shape
    building_count, slot_count = rows.shape
    case_count, axle_count = axle_pos.shape
    block = wave_count // 2
    low_table, high_table = factor_tables(wave_size, wave_count)
    slots = block // STEP + AHEAD
    owned = (case_count // wave_size, building_count // dof_size)
    any_spec = pl.BlockSpec(memory_space=pl.ANY)
    partial_sum = pl.pallas_call(
        functools.partial(kernel, (wave_size, dof_size)),
        out_shape=jax.ShapeDtypeStruct((wave_size * dof_size, *owned), BF16),
        in_specs=[any_spec] * 9,
        out_specs=pl.BlockSpec(memory_space=pltpu.VMEM),
        scratch_shapes=[
            pltpu.VMEM((slots, 2, STEP, force_count, resp), BF16),
            pltpu.VMEM((force_count // 128, 2, wave_count, 128), F32),
            pltpu.VMEM((axle_count, case_count), jnp.int32),
            pltpu.VMEM((axle_count, case_count), F32),
            pltpu.VMEM((slot_count, building_count), jnp.int32),
            pltpu.VMEM((building_count // 128, 128), jnp.int32),
            pltpu.VMEM(coupling.shape, BF16),
            pltpu.VMEM(low_table.shape[1:], F32),
            pltpu.VMEM(high_table.shape[1:], F32),
            pltpu.VMEM((HALF, 2 * wave_count), BF16),
            pltpu.VMEM((HALF, 2 * wave_count), BF16),
            pltpu.VMEM((building_count, GROUP), BF16),
            pltpu.VMEM((building_count, GROUP), BF16),
            pltpu.VMEM((building_count * slot_count // GROUP, GROUP), F32),
            pltpu.VMEM((2, building_count, HALF), BF16),
            pltpu.VMEM((building_count, 2 * wave_count), F32),
            pltpu.VMEM((2, case_count, HALF), F32),
            pltpu.VMEM((2 * case_count, 2 * wave_count), BF16),
            pltpu.VMEM((wave_count, resp), F32),
            pltpu.VMEM((case_count, building_count), F32),
            pltpu.SemaphoreType.DMA((7 + force_count // 128,)),
            pltpu.SemaphoreType.DMA((slots,)),
        ],
        compiler_params=pltpu.CompilerParams(vmem_limit_bytes=60 * 1024 * 1024),
    )(
        green.reshape(2, block, 2, force_count, resp),
        rough,
        axle_pos.T,
        axle_load.T,
        rows.T,
        counts.reshape(building_count // 128, 128),
        coupling,
        jnp.asarray(low_table),
        jnp.asarray(high_table),
    )
    arrived = lax.all_to_all(partial_sum, ("wave", "dof"), 0, 0)
    return jnp.sum(arrived.astype(F32), axis=0).T


def solution(mesh):
    in_specs = (
        P(None, "wave", None, "dof"),
        P(None, "wave", None),
        P(),
        P(),
        P(),
        P(),
        P(None, "dof"),
    )
    out_specs = P("dof", "wave")
    return jax.shard_map(body, mesh=mesh, in_specs=in_specs, out_specs=out_specs, check_vma=False)
```

```python
import functools
import math

import jax
import jax.numpy as jnp
import numpy as np
from jax import lax
from jax.experimental import pallas as pl
from jax.experimental.pallas import tpu as pltpu
from jax.sharding import PartitionSpec as P

K = 2048
HALF = K // 2
LOW = 128
HIGH = HALF // LOW
GROUP = 256
STEP = 8
AHEAD = 6

F32 = jnp.float32
BF16 = jnp.bfloat16


def dot_nn(a, b):
    return lax.dot_general(a, b, (((1,), (0,)), ((), ())), preferred_element_type=F32)


def dot_nt(a, b):
    return lax.dot_general(a, b, (((1,), (1,)), ((), ())), preferred_element_type=F32)


def split(x):
    hi = x.astype(BF16)
    return hi, (x - hi.astype(F32)).astype(BF16)


def iota(shape, axis):
    return lax.broadcasted_iota(jnp.int32, shape, axis)


def factor_tables(wave_size, wave_count):
    block = wave_count // 2

    def one(stations, scale):
        waves = np.arange(wave_size * wave_count).reshape(wave_size, 1, block, 2)
        waves = np.moveaxis(waves, 3, 2)
        angle = (waves * stations[None, :, None, None] % K) * (2.0 * np.pi / K)
        both = np.stack([np.cos(angle), -np.sin(angle)], axis=3) * scale
        return both.reshape(wave_size, len(stations), 2 * wave_count).astype(np.float32)

    return one(np.arange(LOW), 1.0 / math.sqrt(K)), one(np.arange(HIGH) * LOW, 1.0)[:, :, None]


def one_hot_rows(key, weights, dtype):
    zero = jnp.zeros(key.shape, dtype)
    parts = [
        jnp.where(key == jnp.full(key.shape, h + 1, dtype), w, zero)
        for w in weights
        for h in range(2 * HIGH)
    ]
    return jnp.concatenate(parts, axis=0)


def low_rows(row, dtype):
    shape = (LOW, GROUP)
    hit = iota(shape, 0).astype(F32).astype(dtype) == jnp.broadcast_to(row, shape)
    return jnp.where(hit, jnp.ones(shape, dtype), jnp.zeros(shape, dtype))


def spread(values, per_item):
    copies = jnp.where(
        iota((per_item, GROUP), 1) % per_item == iota((per_item, GROUP), 0), 1.0, 0.0
    ).astype(BF16)
    shape = (values.shape[0], GROUP)
    own = iota(shape, 1) // per_item == iota(shape, 0) % (GROUP // per_item)
    return jnp.where(own, dot_nn(values.astype(BF16), copies), 0.0)


def item_sums(values, per_sum):
    rows = values.shape[0]
    shape = (rows // per_sum, rows)
    member = jnp.where(iota(shape, 1) // per_sum == iota(shape, 0), 1.0, 0.0)
    return dot_nn(member.astype(BF16), values.astype(BF16))


def station_parts(x):
    high = lax.shift_right_logical(x, LOW.bit_length() - 1)
    return (high + 1).astype(F32), (x & (LOW - 1)).astype(F32)


def kernel(
    sizes,
    green,
    rough,
    axle_pos,
    axle_load,
    rows,
    counts,
    coupling,
    low_table,
    high_table,
    out,
    ring,
    rough_v,
    pos_v,
    load_v,
    rows_v,
    counts_v,
    coupling_v,
    low_v,
    high_v,
    table_hi,
    table_lo,
    key_v,
    low_key_v,
    key_c_v,
    low_key_c_v,
    load_parts_v,
    occupancy,
    weights_v,
    loads,
    phase_v,
    g_v,
    total,
    small_sem,
    ring_sem,
):
    wave_size, dof_size = sizes
    block, _, _, resp = green.shape[1:]
    slot_count, building_count = rows.shape
    axle_count, case_count = axle_pos.shape
    steps = 2 * block // STEP
    early = 3 * steps // 8
    rounds = building_count // (8 * (GROUP // slot_count))
    assert rounds == HIGH == case_count // (2 * (GROUP // axle_count))
    slots = ring.shape[0]
    wave = lax.axis_index("wave")

    small = [
        pltpu.make_async_copy(src, dst, small_sem.at[i])
        for i, (src, dst) in enumerate(
            [
                (rows, rows_v),
                (counts, counts_v),
                (low_table.at[wave], low_v),
                (high_table.at[wave], high_v),
                (axle_pos, pos_v),
                (axle_load, load_v),
                (coupling, coupling_v),
            ]
            + [
                (rough.at[:, :, t * 128 : (t + 1) * 128], rough_v.at[t])
                for t in range(rough_v.shape[0])
            ]
        )
    ]
    for copy in small:
        copy.start()

    def green_copy(step):
        slot = lax.rem(step, slots)
        per_block = steps // 2
        at = pl.ds(lax.rem(step, per_block) * STEP, STEP)
        return pltpu.make_async_copy(
            green.at[:, at, step // per_block], ring.at[slot], ring_sem.at[slot]
        )

    def pump(step):
        green_copy(step).wait()

        @pl.when(step + AHEAD < steps)
        def _():
            green_copy(step + AHEAD).start()

    for step in range(AHEAD):
        green_copy(jnp.int32(step)).start()
    for copy in small[:2]:
        copy.wait()

    items = GROUP // slot_count
    for k in range(building_count // 128):
        at = slice(128 * k, 128 * (k + 1))
        high, low = station_parts(rows_v[:, at])
        used = iota((slot_count, 128), 0) < counts_v[k : k + 1, :]
        key_v[at, :] = spread(jnp.where(used, high, 0.0).T, slot_count).astype(BF16)
        groups = 128 // items
        low_key_v[groups * k : groups * (k + 1), :] = item_sums(spread(low.T, slot_count), items)
    for copy in small[2:6]:
        copy.wait()
    items_c = GROUP // axle_count
    high, low = station_parts(pos_v[...])
    key_c_v[...] = spread(high.T, axle_count)
    low = item_sums(spread(low.T, axle_count), items_c)
    for r in range(rounds):
        low_key_c_v[r] = low[2 * r : 2 * r + 2]
    for k, part in enumerate(split(load_v[...])):
        load_parts_v[k] = spread(part.astype(F32).T, axle_count)

    @pl.loop(0, rounds, unroll=2)
    def _(r):
        @pl.when(r < early)
        def _():
            pump(r)

        low_eight = low_key_v[pl.ds(pl.multiple_of(r * 8, 8), 8), :]
        for k in range(8):
            at = pl.ds(pl.multiple_of((r * 8 + k) * items, items), items)
            hot = one_hot_rows(key_v[at, :], [jnp.ones((items, GROUP), BF16)], BF16)
            found = dot_nt(hot, low_rows(low_eight[k : k + 1, :].astype(BF16), BF16))
            half = HIGH * items
            both = ((found[:half] + found[half:]).astype(BF16), (found[:half] - found[half:]).astype(BF16))
            for q in range(2):
                for h in range(HIGH):
                    occupancy[q, at, h * LOW : (h + 1) * LOW] = both[q][h * items : (h + 1) * items]

        at = pl.ds(pl.multiple_of(r * LOW, LOW), LOW)
        for q in range(2):
            re = slice(2 * q * block, (2 * q + 1) * block)
            im = slice((2 * q + 1) * block, (2 * q + 2) * block)
            low_re, low_im = low_v[:, re], low_v[:, im]
            high_re, high_im = high_v[r, :, re], high_v[r, :, im]
            table_hi[at, re], table_lo[at, re] = split(low_re * high_re - low_im * high_im)
            table_hi[at, im], table_lo[at, im] = split(low_re * high_im + low_im * high_re)

        low_two = low_key_c_v[r]
        for k in range(2):
            at = pl.ds(pl.multiple_of((2 * r + k) * items_c, items_c), items_c)
            hot = one_hot_rows(key_c_v[at, :], [load_parts_v[0, at, :], load_parts_v[1, at, :]], F32)
            found = dot_nt(hot.astype(BF16), low_rows(low_two[k : k + 1], F32).astype(BF16))
            half = HIGH * items_c
            found = found[: 2 * half] + found[2 * half :]
            both = (found[:half] + found[half:], found[:half] - found[half:])
            for q in range(2):
                for h in range(HIGH):
                    loads[q, at, h * LOW : (h + 1) * LOW] = both[q][h * items_c : (h + 1) * items_c]

    late = list(range(min(rounds, early), early))

    def pump_late(count):
        for step in late[:count]:
            pump(jnp.int32(step))
        del late[:count]

    pump_late(1)

    @pl.loop(0, building_count // 256, unroll=True)
    def _(r):
        at = pl.ds(pl.multiple_of(r * 256, 256), 256)
        for q in range(2):
            cols = slice(2 * q * block, (2 * q + 2) * block)
            weights_v[at, cols] = dot_nn(occupancy[q, at, :], table_hi[:, cols])

    pump_late(1)

    pump_late(1)
    for q in range(2):
        cols = slice(2 * q * block, (2 * q + 2) * block)
        load_hi, load_lo = split(loads[q])
        phase = (
            dot_nn(load_hi, table_hi[:, cols])
            + dot_nn(load_lo, table_hi[:, cols])
            + dot_nn(load_hi, table_lo[:, cols])
        ) * math.sqrt(K / axle_count)
        phase_v[:case_count, cols], phase_v[case_count:, cols] = split(phase)

    for copy in small[6:]:
        copy.wait()

    def one_step(step, q):
        slot = lax.rem(step, slots)
        row = pl.multiple_of((step - q * (steps // 2)) * STEP, STEP)
        at = pl.ds(2 * row + q, STEP, stride=2)
        rough_re, rough_im = (
            jnp.concatenate([rough_v[t, part, at, :] for t in range(rough_v.shape[0])], axis=1)
            for part in range(2)
        )
        re_hi, re_lo = split(rough_re)
        im_hi, im_lo = split(rough_im)
        left = jnp.concatenate(
            [
                jnp.concatenate([a.astype(F32), b.astype(F32)], axis=1)
                for a, b in ((re_hi, -im_hi), (im_hi, re_hi), (re_lo, -im_lo), (im_lo, re_lo))
            ],
            axis=0,
        ).astype(BF16)
        rank = iota((STEP, resp), 0)
        g_re = jnp.zeros((STEP, resp), F32)
        g_im = jnp.zeros((STEP, resp), F32)
        for k in range(STEP):
            right = jnp.concatenate([ring[slot, 0, k], ring[slot, 1, k]], axis=0)
            prod = dot_nn(left, right)
            g_re = jnp.where(rank == k, prod[:STEP] + prod[2 * STEP : 3 * STEP], g_re)
            g_im = jnp.where(rank == k, prod[STEP : 2 * STEP] + prod[3 * STEP :], g_im)
        g_v[q, pl.ds(row, STEP), :] = g_re
        g_v[q, pl.ds(block + row, STEP), :] = g_im

    pump_late(early)
    owned_cases = case_count // wave_size
    owned_buildings = building_count // dof_size
    per_tile = owned_buildings // 128
    for q in range(2):

        def eight_steps(r, q=q):
            for k in range(8):
                if k >= 3:
                    pump(early + 5 * r + k - 3)
                one_step(8 * r + k, q + k // 4 if steps < 16 else q)

        if steps >= 16:
            pl.loop(q * steps // 16, (q + 1) * steps // 16)(eight_steps)
        elif q == 0:
            eight_steps(jnp.int32(0))

        g_both = jnp.concatenate(split(g_v[q]), axis=1)
        re = slice(2 * q * block, (2 * q + 1) * block)
        im = slice((2 * q + 1) * block, (2 * q + 2) * block)
        phase_q = phase_v[:, 2 * q * block : (2 * q + 2) * block]
        for d in range(dof_size):
            at = slice(d * owned_buildings, (d + 1) * owned_buildings)
            coupling_d = coupling_v[at, :]
            h = dot_nt(jnp.concatenate([coupling_d, coupling_d], axis=1), g_both)
            h_re, h_im = h[:, :block], h[:, block:]
            w_re, w_im = weights_v[at, re], weights_v[at, im]
            both = jnp.concatenate([w_re * h_re + w_im * h_im, w_im * h_re - w_re * h_im], axis=1)
            both_hi = both.astype(BF16)
            prod = dot_nt(phase_q, both_hi)
            part = prod[:case_count] + prod[case_count:]
            if q == 0:
                total[:, at] = part
                continue
            count = jnp.concatenate(
                [counts_v[d * per_tile + t : d * per_tile + t + 1, :] for t in range(per_tile)], axis=1
            )
            part = (total[:, at] + part) * (1.0 / count.astype(F32))
            for w in range(wave_size):
                out[w * dof_size + d] = part[w * owned_cases : (w + 1) * owned_cases].astype(BF16)


def body(green, rough, axle_pos, axle_load, rows, counts, coupling):
    wave_size = lax.axis_size("wave")
    dof_size = lax.axis_size("dof")
    _, wave_count, force_count, resp = green.shape
    building_count, slot_count = rows.shape
    case_count, axle_count = axle_pos.shape
    block = wave_count // 2
    low_table, high_table = factor_tables(wave_size, wave_count)
    slots = 3 * wave_count // (8 * STEP) + AHEAD
    owned = (case_count // wave_size, building_count // dof_size)
    any_spec = pl.BlockSpec(memory_space=pl.ANY)
    partial_sum = pl.pallas_call(
        functools.partial(kernel, (wave_size, dof_size)),
        out_shape=jax.ShapeDtypeStruct((wave_size * dof_size, *owned), BF16),
        in_specs=[any_spec] * 9,
        out_specs=pl.BlockSpec(memory_space=pltpu.VMEM),
        scratch_shapes=[
            pltpu.VMEM((slots, 2, STEP, force_count, resp), BF16),
            pltpu.VMEM((force_count // 128, 2, wave_count, 128), F32),
            pltpu.VMEM((axle_count, case_count), jnp.int32),
            pltpu.VMEM((axle_count, case_count), F32),
            pltpu.VMEM((slot_count, building_count), jnp.int32),
            pltpu.VMEM((building_count // 128, 128), jnp.int32),
            pltpu.VMEM(coupling.shape, BF16),
            pltpu.VMEM(low_table.shape[1:], F32),
            pltpu.VMEM(high_table.shape[1:], F32),
            pltpu.VMEM((HALF, 2 * wave_count), BF16),
            pltpu.VMEM((HALF, 2 * wave_count), BF16),
            pltpu.VMEM((building_count, GROUP), BF16),
            pltpu.VMEM((building_count * slot_count // GROUP, GROUP), F32),
            pltpu.VMEM((case_count, GROUP), F32),
            pltpu.VMEM((HIGH, 2, GROUP), F32),
            pltpu.VMEM((2, case_count, GROUP), F32),
            pltpu.VMEM((2, building_count, HALF), BF16),
            pltpu.VMEM((building_count, 2 * wave_count), F32),
            pltpu.VMEM((2, case_count, HALF), F32),
            pltpu.VMEM((2 * case_count, 2 * wave_count), BF16),
            pltpu.VMEM((2, wave_count, resp), F32),
            pltpu.VMEM((case_count, building_count), F32),
            pltpu.SemaphoreType.DMA((7 + force_count // 128,)),
            pltpu.SemaphoreType.DMA((slots,)),
        ],
        compiler_params=pltpu.CompilerParams(vmem_limit_bytes=60 * 1024 * 1024),
    )(
        green.reshape(2, block, 2, force_count, resp),
        rough,
        axle_pos.T,
        axle_load.T,
        rows.T,
        counts.reshape(building_count // 128, 128),
        coupling,
        jnp.asarray(low_table),
        jnp.asarray(high_table),
    )
    arrived = lax.all_to_all(partial_sum, ("wave", "dof"), 0, 0)
    return jnp.sum(arrived.astype(F32), axis=0).T


def solution(mesh):
    in_specs = (
        P(None, "wave", None, "dof"),
        P(None, "wave", None),
        P(),
        P(),
        P(),
        P(),
        P(None, "dof"),
    )
    out_specs = P("dof", "wave")
    return jax.shard_map(body, mesh=mesh, in_specs=in_specs, out_specs=out_specs, check_vma=False)
```

```python
import functools
import math

import jax
import jax.numpy as jnp
import numpy as np
from jax import lax
from jax.experimental import pallas as pl
from jax.experimental.pallas import tpu as pltpu
from jax.sharding import PartitionSpec as P

K = 2048
HALF = K // 2
LOW = 128
HIGH = HALF // LOW
GROUP = 256
STEP = 8
AHEAD = 6

F32 = jnp.float32
BF16 = jnp.bfloat16


def dot_nn(a, b):
    return lax.dot_general(a, b, (((1,), (0,)), ((), ())), preferred_element_type=F32)


def dot_nt(a, b):
    return lax.dot_general(a, b, (((1,), (1,)), ((), ())), preferred_element_type=F32)


def split(x):
    hi = x.astype(BF16)
    return hi, (x - hi.astype(F32)).astype(BF16)


def iota(shape, axis):
    return lax.broadcasted_iota(jnp.int32, shape, axis)


def factor_tables(wave_size, wave_count):
    block = wave_count // 2

    def one(stations, scale):
        waves = np.arange(wave_size * wave_count).reshape(wave_size, 1, block, 2)
        waves = np.moveaxis(waves, 3, 2)
        angle = (waves * stations[None, :, None, None] % K) * (2.0 * np.pi / K)
        both = np.stack([np.cos(angle), -np.sin(angle)], axis=3) * scale
        return both.reshape(wave_size, len(stations), 2 * wave_count).astype(np.float32)

    return one(np.arange(LOW), 1.0 / math.sqrt(K)), one(np.arange(HIGH) * LOW, 1.0)[:, :, None]


def one_hot_rows(key, weights, dtype):
    zero = jnp.zeros(key.shape, dtype)
    parts = [
        jnp.where(key == jnp.full(key.shape, h + 1, dtype), w, zero)
        for w in weights
        for h in range(2 * HIGH)
    ]
    return jnp.concatenate(parts, axis=0)


def low_rows(row, dtype):
    shape = (LOW, GROUP)
    hit = iota(shape, 0).astype(F32).astype(dtype) == jnp.broadcast_to(row, shape)
    return jnp.where(hit, jnp.ones(shape, dtype), jnp.zeros(shape, dtype))


def spread(values, per_item):
    copies = jnp.where(
        iota((per_item, GROUP), 1) % per_item == iota((per_item, GROUP), 0), 1.0, 0.0
    ).astype(BF16)
    shape = (values.shape[0], GROUP)
    own = iota(shape, 1) // per_item == iota(shape, 0) % (GROUP // per_item)
    return jnp.where(own, dot_nn(values.astype(BF16), copies), 0.0)


def item_sums(values, per_sum):
    rows = values.shape[0]
    shape = (rows // per_sum, rows)
    member = jnp.where(iota(shape, 1) // per_sum == iota(shape, 0), 1.0, 0.0)
    return dot_nn(member.astype(BF16), values.astype(BF16))


def station_parts(x):
    high = lax.shift_right_logical(x, LOW.bit_length() - 1)
    return (high + 1).astype(F32), (x & (LOW - 1)).astype(F32)


def kernel(
    sizes,
    green,
    rough,
    axle_pos,
    axle_load,
    rows,
    counts,
    coupling,
    low_table,
    high_table,
    out,
    ring,
    rough_v,
    pos_v,
    load_v,
    rows_v,
    counts_v,
    coupling_v,
    low_v,
    high_v,
    table_hi,
    table_lo,
    key_v,
    low_key_v,
    key_c_v,
    low_key_c_v,
    load_parts_v,
    occupancy,
    weights_v,
    loads,
    phase_v,
    g_v,
    total,
    out_v,
    small_sem,
    ring_sem,
):
    wave_size, dof_size = sizes
    block, _, _, resp = green.shape[1:]
    slot_count, building_count = rows.shape
    axle_count, case_count = axle_pos.shape
    steps = 2 * block // STEP
    early = 3 * steps // 8
    rounds = building_count // (8 * (GROUP // slot_count))
    assert rounds == HIGH == case_count // (2 * (GROUP // axle_count))
    slots = ring.shape[0]
    wave = lax.axis_index("wave")

    small = [
        pltpu.make_async_copy(src, dst, small_sem.at[i])
        for i, (src, dst) in enumerate(
            [
                (rows, rows_v),
                (counts, counts_v),
                (low_table.at[wave], low_v),
                (high_table.at[wave], high_v),
                (axle_pos, pos_v),
                (axle_load, load_v),
                (coupling, coupling_v),
            ]
            + [
                (rough.at[:, :, t * 128 : (t + 1) * 128], rough_v.at[t])
                for t in range(rough_v.shape[0])
            ]
        )
    ]
    for copy in small:
        copy.start()

    def green_copy(step):
        slot = lax.rem(step, slots)
        per_block = steps // 2
        at = pl.ds(lax.rem(step, per_block) * STEP, STEP)
        return pltpu.make_async_copy(
            green.at[:, at, step // per_block], ring.at[slot], ring_sem.at[slot]
        )

    def pump(step):
        green_copy(step).wait()

        @pl.when(step + AHEAD < steps)
        def _():
            green_copy(step + AHEAD).start()

    for step in range(AHEAD):
        green_copy(jnp.int32(step)).start()
    for copy in small[:2]:
        copy.wait()

    items = GROUP // slot_count
    for k in range(building_count // 128):
        at = slice(128 * k, 128 * (k + 1))
        high, low = station_parts(rows_v[:, at])
        used = iota((slot_count, 128), 0) < counts_v[k : k + 1, :]
        key_v[at, :] = spread(jnp.where(used, high, 0.0).T, slot_count).astype(BF16)
        groups = 128 // items
        low_key_v[groups * k : groups * (k + 1), :] = item_sums(spread(low.T, slot_count), items)
    for copy in small[2:6]:
        copy.wait()
    items_c = GROUP // axle_count
    high, low = station_parts(pos_v[...])
    key_c_v[...] = spread(high.T, axle_count)
    low = item_sums(spread(low.T, axle_count), items_c)
    for r in range(rounds):
        low_key_c_v[r] = low[2 * r : 2 * r + 2]
    for k, part in enumerate(split(load_v[...])):
        load_parts_v[k] = spread(part.astype(F32).T, axle_count)

    @pl.loop(0, rounds, unroll=2)
    def _(r):
        @pl.when(r < early)
        def _():
            pump(r)

        low_eight = low_key_v[pl.ds(pl.multiple_of(r * 8, 8), 8), :]
        for k in range(8):
            at = pl.ds(pl.multiple_of((r * 8 + k) * items, items), items)
            hot = one_hot_rows(key_v[at, :], [jnp.ones((items, GROUP), BF16)], BF16)
            found = dot_nt(hot, low_rows(low_eight[k : k + 1, :].astype(BF16), BF16))
            half = HIGH * items
            both = ((found[:half] + found[half:]).astype(BF16), (found[:half] - found[half:]).astype(BF16))
            for q in range(2):
                for h in range(HIGH):
                    occupancy[q, at, h * LOW : (h + 1) * LOW] = both[q][h * items : (h + 1) * items]

        at = pl.ds(pl.multiple_of(r * LOW, LOW), LOW)
        for q in range(2):
            re = slice(2 * q * block, (2 * q + 1) * block)
            im = slice((2 * q + 1) * block, (2 * q + 2) * block)
            low_re, low_im = low_v[:, re], low_v[:, im]
            high_re, high_im = high_v[r, :, re], high_v[r, :, im]
            table_hi[at, re], table_lo[at, re] = split(low_re * high_re - low_im * high_im)
            table_hi[at, im], table_lo[at, im] = split(low_re * high_im + low_im * high_re)

        low_two = low_key_c_v[r]
        for k in range(2):
            at = pl.ds(pl.multiple_of((2 * r + k) * items_c, items_c), items_c)
            hot = one_hot_rows(key_c_v[at, :], [load_parts_v[0, at, :], load_parts_v[1, at, :]], F32)
            found = dot_nt(hot.astype(BF16), low_rows(low_two[k : k + 1], F32).astype(BF16))
            half = HIGH * items_c
            found = found[: 2 * half] + found[2 * half :]
            both = (found[:half] + found[half:], found[:half] - found[half:])
            for q in range(2):
                for h in range(HIGH):
                    loads[q, at, h * LOW : (h + 1) * LOW] = both[q][h * items_c : (h + 1) * items_c]

    late = list(range(min(rounds, early), early))

    def pump_late(count):
        for step in late[:count]:
            pump(jnp.int32(step))
        del late[:count]

    pump_late(1)

    @pl.loop(0, building_count // 256, unroll=True)
    def _(r):
        at = pl.ds(pl.multiple_of(r * 256, 256), 256)
        for q in range(2):
            cols = slice(2 * q * block, (2 * q + 2) * block)
            weights_v[at, cols] = dot_nn(occupancy[q, at, :], table_hi[:, cols])

    pump_late(1)

    pump_late(1)
    for q in range(2):
        cols = slice(2 * q * block, (2 * q + 2) * block)
        load_hi, load_lo = split(loads[q])
        phase = (
            dot_nn(load_hi, table_hi[:, cols])
            + dot_nn(load_lo, table_hi[:, cols])
            + dot_nn(load_hi, table_lo[:, cols])
        ) * math.sqrt(K / axle_count)
        phase_v[:case_count, cols], phase_v[case_count:, cols] = split(phase)

    for copy in small[6:]:
        copy.wait()

    def one_step(step, q):
        slot = lax.rem(step, slots)
        row = pl.multiple_of((step - q * (steps // 2)) * STEP, STEP)
        at = pl.ds(2 * row + q, STEP, stride=2)
        rough_re, rough_im = (
            jnp.concatenate([rough_v[t, part, at, :] for t in range(rough_v.shape[0])], axis=1)
            for part in range(2)
        )
        re_hi, re_lo = split(rough_re)
        im_hi, im_lo = split(rough_im)
        left = jnp.concatenate(
            [
                jnp.concatenate([a.astype(F32), b.astype(F32)], axis=1)
                for a, b in ((re_hi, -im_hi), (im_hi, re_hi), (re_lo, -im_lo), (im_lo, re_lo))
            ],
            axis=0,
        ).astype(BF16)
        rank = iota((STEP, resp), 0)
        g_re = jnp.zeros((STEP, resp), F32)
        g_im = jnp.zeros((STEP, resp), F32)
        for k in range(STEP):
            right = jnp.concatenate([ring[slot, 0, k], ring[slot, 1, k]], axis=0)
            prod = dot_nn(left, right)
            g_re = jnp.where(rank == k, prod[:STEP] + prod[2 * STEP : 3 * STEP], g_re)
            g_im = jnp.where(rank == k, prod[STEP : 2 * STEP] + prod[3 * STEP :], g_im)
        g_v[q, pl.ds(row, STEP), :] = g_re
        g_v[q, pl.ds(block + row, STEP), :] = g_im

    pump_late(early)
    owned_cases = case_count // wave_size

    def out_copy(d):
        return pltpu.make_async_copy(out_v.at[d], out.at[:, d], small_sem.at[d])

    owned_buildings = building_count // dof_size
    per_tile = owned_buildings // 128
    for q in range(2):

        def eight_steps(r, q=q):
            for k in range(8):
                if k >= 3:
                    pump(early + 5 * r + k - 3)
                one_step(8 * r + k, q + k // 4 if steps < 16 else q)

        if steps >= 16:
            pl.loop(q * steps // 16, (q + 1) * steps // 16)(eight_steps)
        elif q == 0:
            eight_steps(jnp.int32(0))

        g_both = jnp.concatenate(split(g_v[q]), axis=1)
        re = slice(2 * q * block, (2 * q + 1) * block)
        im = slice((2 * q + 1) * block, (2 * q + 2) * block)
        phase_q = phase_v[:, 2 * q * block : (2 * q + 2) * block]
        for d in range(dof_size):
            at = slice(d * owned_buildings, (d + 1) * owned_buildings)
            coupling_d = coupling_v[at, :]
            h = dot_nt(jnp.concatenate([coupling_d, coupling_d], axis=1), g_both)
            h_re, h_im = h[:, :block], h[:, block:]
            w_re, w_im = weights_v[at, re], weights_v[at, im]
            both = jnp.concatenate([w_re * h_re + w_im * h_im, w_im * h_re - w_re * h_im], axis=1)
            both_hi = both.astype(BF16)
            prod = dot_nt(phase_q, both_hi)
            part = prod[:case_count] + prod[case_count:]
            if q == 0:
                total[:, at] = part
                continue
            count = jnp.concatenate(
                [counts_v[d * per_tile + t : d * per_tile + t + 1, :] for t in range(per_tile)], axis=1
            )
            part = (total[:, at] + part) * (1.0 / count.astype(F32))
            for w in range(wave_size):
                out_v[d, w] = part[w * owned_cases : (w + 1) * owned_cases].astype(BF16)
            out_copy(d).start()
    for d in range(dof_size):
        out_copy(d).wait()


def body(green, rough, axle_pos, axle_load, rows, counts, coupling):
    wave_size = lax.axis_size("wave")
    dof_size = lax.axis_size("dof")
    _, wave_count, force_count, resp = green.shape
    building_count, slot_count = rows.shape
    case_count, axle_count = axle_pos.shape
    block = wave_count // 2
    low_table, high_table = factor_tables(wave_size, wave_count)
    slots = 3 * wave_count // (8 * STEP) + AHEAD
    owned = (case_count // wave_size, building_count // dof_size)
    any_spec = pl.BlockSpec(memory_space=pl.ANY)
    partial_sum = pl.pallas_call(
        functools.partial(kernel, (wave_size, dof_size)),
        out_shape=jax.ShapeDtypeStruct((wave_size, dof_size, *owned), BF16),
        in_specs=[any_spec] * 9,
        out_specs=any_spec,
        scratch_shapes=[
            pltpu.VMEM((slots, 2, STEP, force_count, resp), BF16),
            pltpu.VMEM((force_count // 128, 2, wave_count, 128), F32),
            pltpu.VMEM((axle_count, case_count), jnp.int32),
            pltpu.VMEM((axle_count, case_count), F32),
            pltpu.VMEM((slot_count, building_count), jnp.int32),
            pltpu.VMEM((building_count // 128, 128), jnp.int32),
            pltpu.VMEM(coupling.shape, BF16),
            pltpu.VMEM(low_table.shape[1:], F32),
            pltpu.VMEM(high_table.shape[1:], F32),
            pltpu.VMEM((HALF, 2 * wave_count), BF16),
            pltpu.VMEM((HALF, 2 * wave_count), BF16),
            pltpu.VMEM((building_count, GROUP), BF16),
            pltpu.VMEM((building_count * slot_count // GROUP, GROUP), F32),
            pltpu.VMEM((case_count, GROUP), F32),
            pltpu.VMEM((HIGH, 2, GROUP), F32),
            pltpu.VMEM((2, case_count, GROUP), F32),
            pltpu.VMEM((2, building_count, HALF), BF16),
            pltpu.VMEM((building_count, 2 * wave_count), F32),
            pltpu.VMEM((2, case_count, HALF), F32),
            pltpu.VMEM((2 * case_count, 2 * wave_count), BF16),
            pltpu.VMEM((2, wave_count, resp), F32),
            pltpu.VMEM((case_count, building_count), F32),
            pltpu.VMEM((dof_size, wave_size, *owned), BF16),
            pltpu.SemaphoreType.DMA((7 + force_count // 128,)),
            pltpu.SemaphoreType.DMA((slots,)),
        ],
        compiler_params=pltpu.CompilerParams(vmem_limit_bytes=60 * 1024 * 1024),
    )(
        green.reshape(2, block, 2, force_count, resp),
        rough,
        axle_pos.T,
        axle_load.T,
        rows.T,
        counts.reshape(building_count // 128, 128),
        coupling,
        jnp.asarray(low_table),
        jnp.asarray(high_table),
    )
    arrived = lax.all_to_all(
        partial_sum.reshape(wave_size * dof_size, *owned), ("wave", "dof"), 0, 0
    )
    return jnp.sum(arrived.astype(F32), axis=0).T


def solution(mesh):
    in_specs = (
        P(None, "wave", None, "dof"),
        P(None, "wave", None),
        P(),
        P(),
        P(),
        P(),
        P(None, "dof"),
    )
    out_specs = P("dof", "wave")
    return jax.shard_map(body, mesh=mesh, in_specs=in_specs, out_specs=out_specs, check_vma=False)
```
